32 devices in a mesh: req: 8 (over y, x, core), tp: 4 (over z).
Axes of the slice: x: 2, y: 2, z: 4, core: 2. Of those that a mesh axis runs over, the one named last changes fastest.
Arguments:
- hidden_in: bfloat16 [8192, 2048], P('req'), may hold values from -6 to 6
- norm_gain: bfloat16 [2048], replicated, may hold values from 0.099609375 to 1.8984375
- w_query: bfloat16 [2048, 1280], P(None, 'tp'), may hold values from -0.125 to 0.125
- key_value_weight: bfloat16 [2048, 640], replicated, may hold values from -0.3125 to 0.3125
- w_out: bfloat16 [1280, 2048], replicated, may hold values from -0.625 to 0.625
- prior_cache: bfloat16 [8, 7168, 640], P('req'), may hold values from -52 to 52
- cache_len: int32 [8], P('req'), may hold values from 1 to 7168, 28672 in all
- group_len: int32 [8], P('req'), may hold values from 1 to 1024, 4096 in all
- page_map: int32 [8, 32], P('req'), may hold values from 0 to 31, each once within a row
Outputs:
- hidden_out: bfloat16 [8192, 2048], P(('req', 'tp'))
- decode_kv: bfloat16 [32, 8, 256, 640], P(('req', 'tp'))
The draws below stay inside these ranges and needn't reach their ends.
Inputs may be any that keep to these rules, and one draw needn't show every extreme that they name: `page_map`: each row names every device index once.
All inputs are finite; a program needn't handle non-finite values. No bound on the sum of `cache_len` or of `group_len` on one device may be relied on, other than what follows from the above.
Results may differ from the reference program's by a relative error of at most 0.014.
The reference program's roundings to bfloat16 on the way count: a program that leaves them out, or rounds other values in their place, can miss the bound.
Values may be sent and summed in bfloat16 or wider, within the bound.
A program may use at most 128 MiB of HBM per device.

```python
import math
import jax
import jax.numpy as jnp
import numpy as np
from jax import lax

MODEL_WIDTH = 2048
QUERY_HEAD_COUNT = 20
KEY_VALUE_HEADS = 5
HEAD_SIZE = 64
NEW_TOKEN_SLOTS = 1024
PRIOR_SLOTS = 7168
KEYS_PER_BLOCK = 512
REQUEST_TOTAL = 8
TOKENS = 8192
N_REQ = 8
N_TP = 4
DEVICES = 32


def draw_prior_cache(key, part):
    array_shape = (REQUEST_TOTAL, PRIOR_SLOTS, 2 * KEY_VALUE_HEADS * HEAD_SIZE)
    first_key = jax.random.fold_in(key, 11)
    values = jnp.clip(2.5 * jax.random.normal(first_key, array_shape, jnp.float32), -10.0, 10.0)
    return values.astype(jnp.bfloat16)


def levels(own_key, dims, split, least, largest):
    level, own = 1.0, jax.random.fold_in(own_key, 6)
    for axis_at, blocks in split:
        steps = jnp.exp(jax.random.uniform(jax.random.fold_in(own, axis_at), (blocks,), jnp.float32, least / len(split), largest / len(split)))
        level = level * jnp.repeat(steps, dims[axis_at] // blocks).reshape([-1 if axis == axis_at else 1 for axis in range(len(dims))])
    return level


def split_up(number_of, total, most, skew):
    weights = [(1 << 20) // math.isqrt(rank ** skew) + 1 for rank in range(2, number_of + 1)]
    spare, counts = total - most - (number_of - 1), [1] * (number_of - 1)
    while spare > 0:
        candidates = [i for i in range(number_of - 1) if counts[i] < most]
        pool, remaining = sum([weights[i] for i in candidates]), spare
        for i in candidates:
            more = min(most - counts[i], max(1, remaining * weights[i] // pool), spare)
            counts[i] = counts[i] + more
            spare = spare - more
    return np.array([most] + counts)


def uneven(own_key, count, total, most, slope):
    if count == 2:
        one = jax.random.randint(own_key, (), max(1, total - most), min(most, total - 1) + 1)
        return jnp.stack([one, total - one])
    tallies = jnp.asarray(split_up(count, total, most, slope), jnp.int32)
    couples = (count - 1) // 2
    giver, sink = tallies[1:1 + 2 * couples:2], tallies[2:2 + 2 * couples:2]
    margin = jnp.minimum(giver - 1, most - sink)
    shifted = jax.random.randint(jax.random.fold_in(own_key, 1), (couples,), 0, 1 << 20) % (margin + 1)
    tallies = tallies.at[1:1 + 2 * couples:2].set(giver - shifted).at[2:2 + 2 * couples:2].set(sink + shifted)
    return tallies[jax.random.permutation(jax.random.fold_in(own_key, 2), count)]


def bell_draw(key, extent, width, reach, split=(), kind=jnp.bfloat16):
    gain = levels(key, extent, split, -0.22, 0.18) if split else 1.0
    array = jax.random.normal(key, extent, jnp.float32) * width * gain
    return jnp.minimum(jnp.maximum(array, -reach), reach).astype(kind)


def setup_inputs(seed: int = 0) -> dict:
    seeds = jax.random.split(jax.random.key(seed), 10)
    hidden_in = bell_draw(seeds[0], (TOKENS, MODEL_WIDTH), 1.0, 6.0, ((0, 8),))
    norm_gain = jnp.clip(1.0 + 0.18 * jax.random.normal(seeds[1], (MODEL_WIDTH,), jnp.float32), 0.099609375, 1.8984375).astype(jnp.bfloat16)
    w_query = bell_draw(seeds[2], (MODEL_WIDTH, QUERY_HEAD_COUNT * HEAD_SIZE), MODEL_WIDTH ** -0.5, 0.125, ((1, 4),))
    key_value_weight = bell_draw(seeds[3], (MODEL_WIDTH, 2 * KEY_VALUE_HEADS * HEAD_SIZE), (MODEL_WIDTH // 6) ** -0.5, 0.3125)
    w_out = bell_draw(seeds[4], (QUERY_HEAD_COUNT * HEAD_SIZE, MODEL_WIDTH), (QUERY_HEAD_COUNT * HEAD_SIZE // 16) ** -0.5, 0.625)
    prior_cache = draw_prior_cache(jax.random.fold_in(seeds[9], 71), 0)
    cache_len = uneven(seeds[6], REQUEST_TOTAL, REQUEST_TOTAL * PRIOR_SLOTS // 2, PRIOR_SLOTS, 2).astype(jnp.int32)
    group_len = uneven(seeds[7], REQUEST_TOTAL, REQUEST_TOTAL * NEW_TOKEN_SLOTS // 2, NEW_TOKEN_SLOTS, 2).astype(jnp.int32)
    page_map = jax.vmap(lambda own: jax.random.permutation(own, DEVICES))(jax.random.split(seeds[8], REQUEST_TOTAL)).reshape((REQUEST_TOTAL, DEVICES)).astype(jnp.int32)
    return dict(hidden_in=hidden_in, norm_gain=norm_gain, w_query=w_query, key_value_weight=key_value_weight, w_out=w_out, prior_cache=prior_cache, cache_len=cache_len, group_len=group_len, page_map=page_map)


def rotation_table(values, token_positions, heads):
    half_size = HEAD_SIZE // 2
    frequency = 10000.0 ** (-(jnp.arange(half_size, dtype=jnp.float32) * 2.0 / HEAD_SIZE))
    angles = token_positions.astype(jnp.float32)[:, None] * frequency[None, :]
    cosine = jnp.cos(angles)[:, None, :]
    sine_part = jnp.sin(angles)[:, None, :]
    shaped = values.reshape(values.shape[0], heads, HEAD_SIZE)
    first_half = shaped[..., :half_size]
    second_half = shaped[..., half_size:]
    turned = jnp.concatenate([first_half * cosine - second_half * sine_part, second_half * cosine + first_half * sine_part], axis=-1)
    return turned.reshape(values.shape)

def flash_step(carry, start, queries, every_key, every_value, cached, fresh, row_ids):
    top_score, denom_sum, weighted = carry
    key_tile = lax.dynamic_slice_in_dim(every_key, start, KEYS_PER_BLOCK, 0).astype(jnp.float32)
    value_tile = lax.dynamic_slice_in_dim(every_value, start, KEYS_PER_BLOCK, 0).astype(jnp.float32)
    columns = start + jnp.arange(KEYS_PER_BLOCK, dtype=jnp.int32)
    later = columns[None, :] - PRIOR_SLOTS
    allowed = (columns[None, :] < cached) | (later >= 0) & (later <= row_ids[:, None]) & (later < fresh)
    scores = jnp.einsum('qhd,khd->qhk', queries, key_tile) * HEAD_SIZE ** (-0.5)
    scores = jnp.where(allowed[:, None, :], scores, -1e+30)
    new_top = jnp.maximum(top_score, lax.optimization_barrier(jnp.max(scores, axis=-1)))
    rescale = jnp.exp(top_score - new_top)
    chances = jnp.where(allowed[:, None, :], jnp.exp(scores - new_top[..., None]), 0.0).astype(jnp.bfloat16)
    chances_wide = lax.optimization_barrier(chances).astype(jnp.float32)
    denom_sum = denom_sum * rescale + lax.optimization_barrier(jnp.sum(chances_wide, axis=-1))
    weighted = weighted * rescale[..., None] + jnp.einsum('qhk,khd->qhd', chances_wide, value_tile)
    return (new_top, denom_sum, weighted)

def reference(hidden_in, norm_gain, w_query, key_value_weight, w_out, prior_cache, cache_len, group_len, page_map):
    key_span_width = KEY_VALUE_HEADS * HEAD_SIZE
    device_count = N_REQ * N_TP
    block_rows = (PRIOR_SLOTS + NEW_TOKEN_SLOTS) // device_count

    def one_request(items):
        tokens, cache_rows, cached, fresh, mapping = items
        hidden = tokens.astype(jnp.float32)
        normed = (hidden * lax.rsqrt(lax.optimization_barrier(jnp.mean(hidden * hidden, axis=-1, keepdims=True)) + 1e-05) * norm_gain.astype(jnp.float32)).astype(jnp.bfloat16)
        row_ids = jnp.arange(NEW_TOKEN_SLOTS, dtype=jnp.int32)
        token_positions = cached + row_ids
        queries = rotation_table(jnp.dot(normed, w_query, preferred_element_type=jnp.float32), token_positions, QUERY_HEAD_COUNT).astype(jnp.bfloat16)
        unrotated_input = jnp.dot(normed, key_value_weight, preferred_element_type=jnp.float32)
        key_value_rows = jnp.concatenate([rotation_table(unrotated_input[:, :key_span_width], token_positions, KEY_VALUE_HEADS), unrotated_input[:, key_span_width:]], axis=1).astype(jnp.bfloat16)
        zero = jnp.zeros((), jnp.bfloat16)
        old_part = jnp.where((jnp.arange(PRIOR_SLOTS, dtype=jnp.int32) < cached)[:, None], cache_rows, zero)
        new_part = jnp.where((row_ids < fresh)[:, None], key_value_rows, zero)
        context_output = jnp.concatenate([old_part, new_part], axis=0)
        every_key = jnp.repeat(context_output[:, :key_span_width].reshape(PRIOR_SLOTS + NEW_TOKEN_SLOTS, KEY_VALUE_HEADS, HEAD_SIZE), QUERY_HEAD_COUNT // KEY_VALUE_HEADS, axis=1)
        every_value = jnp.repeat(context_output[:, key_span_width:].reshape(PRIOR_SLOTS + NEW_TOKEN_SLOTS, KEY_VALUE_HEADS, HEAD_SIZE), QUERY_HEAD_COUNT // KEY_VALUE_HEADS, axis=1)
        query_heads = queries.reshape(NEW_TOKEN_SLOTS, QUERY_HEAD_COUNT, HEAD_SIZE).astype(jnp.float32)
        initial = (jnp.full((NEW_TOKEN_SLOTS, QUERY_HEAD_COUNT), -1e+30, jnp.float32), jnp.zeros((NEW_TOKEN_SLOTS, QUERY_HEAD_COUNT), jnp.float32), jnp.zeros((NEW_TOKEN_SLOTS, QUERY_HEAD_COUNT, HEAD_SIZE), jnp.float32))

        def scan_step(carry, start):
            return (flash_step(carry, start, query_heads, every_key, every_value, cached, fresh, row_ids), None)
        starts = jnp.arange((PRIOR_SLOTS + NEW_TOKEN_SLOTS) // KEYS_PER_BLOCK, dtype=jnp.int32) * KEYS_PER_BLOCK
        final, unused = lax.scan(scan_step, initial, starts)
        heads_out = (final[2] / final[1][..., None]).astype(jnp.bfloat16).reshape(NEW_TOKEN_SLOTS, QUERY_HEAD_COUNT * HEAD_SIZE)
        mixed = jnp.dot(heads_out, w_out, preferred_element_type=jnp.float32)
        result = jnp.where((row_ids < fresh)[:, None], hidden + mixed, 0.0).astype(jnp.bfloat16)
        inverse = jnp.argsort(mapping).astype(jnp.int32)
        blocks = context_output.reshape(device_count, block_rows, 2 * key_span_width)[inverse]
        return (result, blocks)
    results, blocks = lax.map(one_request, (hidden_in.reshape(REQUEST_TOTAL, NEW_TOKEN_SLOTS, MODEL_WIDTH), prior_cache, cache_len, group_len, page_map))
    return (results.reshape(REQUEST_TOTAL * NEW_TOKEN_SLOTS, MODEL_WIDTH), jnp.transpose(blocks, (1, 0, 2, 3)))
```

```python
import functools

import jax
import jax.numpy as jnp
from jax import lax
from jax.experimental import pallas as pl
from jax.experimental.pallas import tpu as pltpu
from jax.sharding import PartitionSpec as P

QUERY_HEAD_COUNT = 20
KEY_VALUE_HEADS = 5
HEAD_SIZE = 64
NEW_TOKEN_SLOTS = 1024
PRIOR_SLOTS = 7168
KEY_WIDTH = KEY_VALUE_HEADS * HEAD_SIZE
KEYS = 512
TILE = 256
PAIR = 2 * HEAD_SIZE
VALUE_ROWS = 80
VMEM_BYTES = 50 * 1024 * 1024


def rotate_columns(turned, positions, heads):
    half = HEAD_SIZE // 2
    frequency = 10000.0 ** (-(jnp.arange(half, dtype=jnp.float32) * 2.0 / HEAD_SIZE))
    angles = frequency[:, None] * positions.astype(jnp.float32)[None, :]
    cosine, sine = jnp.cos(angles)[None], jnp.sin(angles)[None]
    shaped = turned.reshape(heads, 2, half, turned.shape[1])
    first, second = shaped[:, 0], shaped[:, 1]
    return jnp.stack(
        [first * cosine - second * sine, second * cosine + first * sine], axis=1
    ).reshape(turned.shape)


def ship_kernel(block_rows, prior_blocks, picks, sizes, prior_ref, fresh_ref, out_ref):
    pick = picks[pl.program_id(0)]
    is_prior = pick < prior_blocks
    base = jnp.where(is_prior, pick, pick - prior_blocks) * block_rows
    live = jnp.where(is_prior, sizes[0], sizes[1])
    row = base + lax.broadcasted_iota(jnp.int32, (block_rows, 1), 0)
    zero = jnp.zeros((), jnp.bfloat16)

    @pl.when(is_prior)
    def _():
        out_ref[0] = jnp.where(row < live, prior_ref[...], zero)

    @pl.when(jnp.logical_not(is_prior))
    def _():
        out_ref[0] = jnp.where(row < live, fresh_ref[...], zero)


def pick_blocks(picks, sizes, prior, fresh, block_rows):
    prior_blocks = prior.shape[0] // block_rows
    width = prior.shape[1]
    return pl.pallas_call(
        functools.partial(ship_kernel, block_rows, prior_blocks),
        grid_spec=pltpu.PrefetchScalarGridSpec(
            num_scalar_prefetch=2,
            grid=(picks.shape[0],),
            in_specs=[
                pl.BlockSpec(
                    (block_rows, width),
                    lambda i, picks, sizes: (jnp.minimum(picks[i], prior_blocks - 1), 0),
                ),
                pl.BlockSpec(
                    (block_rows, width),
                    lambda i, picks, sizes: (jnp.maximum(picks[i] - prior_blocks, 0), 0),
                ),
            ],
            out_specs=pl.BlockSpec((1, block_rows, width), lambda i, picks, sizes: (i, 0, 0)),
        ),
        out_shape=jax.ShapeDtypeStruct((picks.shape[0], block_rows, width), jnp.bfloat16),
    )(picks, sizes, prior, fresh)


def attention_kernel(
    heads, sizes, q_ref, prior_ref, fresh_ref, out_ref, staged, keys, values, q_pair, top, acc, sems
):
    cached, fresh, first_kv = sizes[0], sizes[1], sizes[2]
    split = sizes[3]
    tiles = (fresh + TILE - 1) // TILE
    prior_live = (cached + KEYS - 1) // KEYS
    prior_whole = cached // KEYS
    remainder = cached - prior_whole * KEYS

    def fetch(block):
        rows = pl.ds(pl.multiple_of(block * KEYS, KEYS), KEYS)
        return pltpu.make_async_copy(prior_ref.at[rows], staged.at[rows], sems.at[block])

    @pl.loop(0, prior_live)
    def _(block):
        fetch(block).start()

    key_start = first_kv * HEAD_SIZE
    row_in = lax.broadcasted_iota(jnp.int32, (2 * KEY_WIDTH, PAIR), 0)
    lane_in = lax.broadcasted_iota(jnp.int32, (2 * KEY_WIDTH, PAIR), 1)
    choose_keys = (row_in == lane_in + key_start).astype(jnp.float32).astype(jnp.bfloat16)
    row_out = lax.broadcasted_iota(jnp.int32, (PAIR, 2 * KEY_WIDTH), 0)
    lane_out = lax.broadcasted_iota(jnp.int32, (PAIR, 2 * KEY_WIDTH), 1)
    choose_values = (
        (lane_out == row_out + key_start + KEY_WIDTH).astype(jnp.float32).astype(jnp.bfloat16)
    )

    def unpack(rows, at, count):
        keys[pl.ds(at, count), :] = jnp.dot(
            rows, choose_keys, preferred_element_type=jnp.float32
        ).astype(jnp.bfloat16)
        turned = lax.dot_general(
            choose_values, rows, (((1,), (1,)), ((), ())), preferred_element_type=jnp.float32
        ).astype(jnp.bfloat16)
        ones = jnp.ones((VALUE_ROWS - HEAD_SIZE, count), jnp.bfloat16)
        for half in range(2):
            values[half, :HEAD_SIZE, pl.ds(at, count)] = turned[
                half * HEAD_SIZE : (half + 1) * HEAD_SIZE
            ]
            values[half, HEAD_SIZE:, pl.ds(at, count)] = ones

    @pl.loop(0, tiles)
    def _(tile):
        rows = pl.ds(pl.multiple_of(tile * TILE, TILE), TILE)
        unpack(fresh_ref[rows, :], pl.multiple_of(PRIOR_SLOTS + tile * TILE, TILE), TILE)

    @pl.loop(0, prior_live)
    def _(block):
        fetch(block).wait()
        at = pl.multiple_of(block * KEYS, KEYS)
        unpack(staged[pl.ds(at, KEYS), :], at, KEYS)

    out_ref[...] = jnp.zeros_like(out_ref)

    def step(at, count, allowed):
        key_block = keys[pl.ds(at, count), :]

        def score(head):
            return jnp.dot(key_block, q_pair[head], preferred_element_type=jnp.float32)

        ahead = score(0)
        for head in range(heads):
            scores = ahead
            if head + 1 < heads:
                ahead = score(head + 1)
            if allowed is not None:
                scores = jnp.where(allowed, scores, -1e30)
            old = top[head]
            new = jnp.maximum(old, jnp.max(scores, axis=0, keepdims=True))
            top[head] = new
            chances = jnp.exp(scores - new).astype(jnp.bfloat16)
            group = jnp.where(head < split, 0, 1)
            acc[head] = acc[head] * jnp.exp(old - new) + jnp.dot(
                values[group, :, pl.ds(at, count)], chances, preferred_element_type=jnp.float32
            )

    @pl.loop(0, tiles)
    def _(tile):
        columns = pl.ds(pl.multiple_of(tile * TILE, TILE), TILE)
        for head in range(heads):
            query = q_ref[head, :, columns]
            none = jnp.zeros_like(query)
            lower = head < split
            q_pair[head, :HEAD_SIZE] = jnp.where(lower, query, none)
            q_pair[head, HEAD_SIZE:] = jnp.where(lower, none, query)
        top[...] = jnp.full_like(top, -1e30)
        acc[...] = jnp.zeros_like(acc)

        @pl.loop(0, prior_whole)
        def _(block):
            step(pl.multiple_of(block * KEYS, KEYS), KEYS, None)

        @pl.when(remainder > 0)
        def _():
            index = lax.broadcasted_iota(jnp.int32, (KEYS, TILE), 0)
            step(pl.multiple_of(prior_whole * KEYS, KEYS), KEYS, index < remainder)

        @pl.loop(0, tile)
        def _(block):
            step(pl.multiple_of(PRIOR_SLOTS + block * TILE, TILE), TILE, None)

        index = lax.broadcasted_iota(jnp.int32, (TILE, TILE), 0)
        slot = lax.broadcasted_iota(jnp.int32, (TILE, TILE), 1)
        step(pl.multiple_of(PRIOR_SLOTS + tile * TILE, TILE), TILE, index <= slot)
        for head in range(heads):
            total = acc[head]
            out_ref[tile, head * HEAD_SIZE : (head + 1) * HEAD_SIZE, :] = (
                total[:HEAD_SIZE] / total[HEAD_SIZE : HEAD_SIZE + 1]
            ).astype(jnp.bfloat16)


def attention(sizes, queries, prior, fresh_rows):
    heads = queries.shape[0]
    tiles = NEW_TOKEN_SLOTS // TILE
    context = PRIOR_SLOTS + NEW_TOKEN_SLOTS
    return pl.pallas_call(
        functools.partial(attention_kernel, heads),
        in_specs=[
            pl.BlockSpec(memory_space=pltpu.SMEM),
            pl.BlockSpec(memory_space=pltpu.VMEM),
            pl.BlockSpec(memory_space=pl.ANY),
            pl.BlockSpec(memory_space=pltpu.VMEM),
        ],
        out_specs=pl.BlockSpec(memory_space=pltpu.VMEM),
        out_shape=jax.ShapeDtypeStruct((tiles, heads * HEAD_SIZE, TILE), jnp.bfloat16),
        scratch_shapes=[
            pltpu.VMEM((PRIOR_SLOTS, 2 * KEY_WIDTH), jnp.bfloat16),
            pltpu.VMEM((context, PAIR), jnp.bfloat16),
            pltpu.VMEM((2, VALUE_ROWS, context), jnp.bfloat16),
            pltpu.VMEM((heads, PAIR, TILE), jnp.bfloat16),
            pltpu.VMEM((heads, 1, TILE), jnp.float32),
            pltpu.VMEM((heads, VALUE_ROWS, TILE), jnp.float32),
            pltpu.SemaphoreType.DMA((PRIOR_SLOTS // KEYS,)),
        ],
        compiler_params=pltpu.CompilerParams(vmem_limit_bytes=VMEM_BYTES),
        cost_estimate=pl.CostEstimate(
            flops=4 * NEW_TOKEN_SLOTS * heads * context * PAIR,
            bytes_accessed=2 * context * 2 * KEY_WIDTH,
            transcendentals=NEW_TOKEN_SLOTS * heads * context,
        ),
    )(sizes, queries, prior, fresh_rows)


def shards(
    hidden_in,
    norm_gain,
    w_query,
    key_value_weight,
    w_out,
    prior_cache,
    cache_len,
    group_len,
    page_map,
):
    rank = lax.axis_index("tp")
    tp_count = lax.axis_size("tp")
    req_count = lax.axis_size("req")
    span = hidden_in.shape[0] // tp_count
    heads = w_query.shape[1] // HEAD_SIZE
    blocks = page_map.shape[1]
    block_rows = (PRIOR_SLOTS + NEW_TOKEN_SLOTS) // blocks
    cached, fresh = cache_len[0], group_len[0]

    hidden = hidden_in.astype(jnp.float32)
    normed = (
        hidden
        * lax.rsqrt(jnp.mean(hidden * hidden, axis=-1, keepdims=True) + 1e-05)
        * norm_gain.astype(jnp.float32)
    ).astype(jnp.bfloat16)
    slots = jnp.arange(NEW_TOKEN_SLOTS, dtype=jnp.int32)
    positions = cached + slots

    def project(weight):
        return lax.dot_general(
            weight, normed, (((0,), (1,)), ((), ())), preferred_element_type=jnp.float32
        )

    keyval = project(key_value_weight)
    keyval = jnp.concatenate(
        [rotate_columns(keyval[:KEY_WIDTH], positions, KEY_VALUE_HEADS), keyval[KEY_WIDTH:]], axis=0
    ).astype(jnp.bfloat16)
    fresh_rows = keyval.T

    targets = jnp.arange(req_count, dtype=jnp.int32) * tp_count + rank
    picks = jnp.sum(
        jnp.where(
            page_map[0][None, :] == targets[:, None],
            jnp.arange(blocks, dtype=jnp.int32)[None, :],
            0,
        ),
        axis=1,
    ).astype(jnp.int32)
    first_head = rank * heads
    group = QUERY_HEAD_COUNT // KEY_VALUE_HEADS
    first_kv = first_head // group
    split = (first_kv + 1) * group - first_head
    sizes = jnp.stack([cached, fresh, first_kv, split]).astype(jnp.int32)

    shipment = pick_blocks(picks, sizes, prior_cache[0], fresh_rows, block_rows)
    decode_kv = lax.all_to_all(shipment, "req", split_axis=0, concat_axis=0, tiled=True)[None]

    queries = rotate_columns(project(w_query), positions, heads).astype(jnp.bfloat16)
    queries = (queries * HEAD_SIZE ** (-0.5)).astype(jnp.bfloat16)
    attended = attention(
        sizes, queries.reshape(heads, HEAD_SIZE, NEW_TOKEN_SLOTS), prior_cache[0], fresh_rows
    )
    gathered = lax.all_to_all(attended, "tp", split_axis=0, concat_axis=0, tiled=True)
    mixed = lax.dot_general(
        gathered.reshape(QUERY_HEAD_COUNT * HEAD_SIZE, span),
        w_out,
        (((0,), (0,)), ((), ())),
        preferred_element_type=jnp.float32,
    )
    live = rank * span + jnp.arange(span, dtype=jnp.int32) < fresh
    own = lax.dynamic_slice_in_dim(hidden_in, rank * span, span, 0).astype(jnp.float32)
    hidden_out = jnp.where(live[:, None], own + mixed, 0.0).astype(jnp.bfloat16)
    return (hidden_out, decode_kv)


def solution(mesh):
    placed = (
        P("req", None),
        P(),
        P(None, "tp"),
        P(),
        P(),
        P("req", None, None),
        P("req"),
        P("req"),
        P("req", None),
    )
    return jax.shard_map(
        shards,
        mesh=mesh,
        in_specs=placed,
        out_specs=(P(("req", "tp"), None), P(("req", "tp"), None, None, None)),
        check_vma=False,
    )
```

```python
import functools
import math

import jax
import jax.numpy as jnp
from jax import lax
from jax.experimental import pallas as pl
from jax.experimental.pallas import tpu as pltpu
from jax.sharding import PartitionSpec as P

QUERY_HEAD_COUNT = 20
KEY_VALUE_HEADS = 5
HEAD_SIZE = 64
NEW_TOKEN_SLOTS = 1024
PRIOR_SLOTS = 7168
KEY_WIDTH = KEY_VALUE_HEADS * HEAD_SIZE
KEYS = 512
TILE = 256
PAIR = 2 * HEAD_SIZE
VALUE_ROWS = 80
LANES = 128
QUERY_SCALE = HEAD_SIZE ** (-0.5) * math.log2(math.e)
VMEM_BYTES = 50 * 1024 * 1024


def project_kernel(
    hidden_ref, gain_ref, query_weight_ref, keyval_weight_ref, cosine_ref, sine_ref, q_ref, kv_ref
):
    half = HEAD_SIZE // 2
    hidden = hidden_ref[...].astype(jnp.float32)
    normed = (
        hidden
        * lax.rsqrt(jnp.mean(hidden * hidden, axis=-1, keepdims=True) + 1e-05)
        * gain_ref[...].astype(jnp.float32)
    ).astype(jnp.bfloat16)
    cosine, sine = cosine_ref[...], sine_ref[...]

    turned = lax.dot_general(
        query_weight_ref[...], normed, (((1,), (1,)), ((), ())), preferred_element_type=jnp.float32
    )
    for head in range(q_ref.shape[0]):
        first = turned[head * HEAD_SIZE : head * HEAD_SIZE + half]
        second = turned[head * HEAD_SIZE + half : (head + 1) * HEAD_SIZE]
        q_ref[head, :half] = ((first * cosine - second * sine) * QUERY_SCALE).astype(jnp.bfloat16)
        q_ref[head, half:] = ((second * cosine + first * sine) * QUERY_SCALE).astype(jnp.bfloat16)

    keyval = jnp.dot(normed, keyval_weight_ref[...], preferred_element_type=jnp.float32)
    covered = (KEY_WIDTH + LANES - 1) // LANES * LANES
    repeat = LANES // half
    lanes_cosine = jnp.concatenate([jnp.concatenate([cosine] * repeat, axis=0).T] * (covered // LANES), axis=1)
    lanes_sine = jnp.concatenate([jnp.concatenate([sine] * repeat, axis=0).T] * (covered // LANES), axis=1)
    start = keyval[:, :covered]
    lane = lax.broadcasted_iota(jnp.int32, start.shape, 1)
    swapped = jnp.where(
        lane % HEAD_SIZE < half,
        -pltpu.roll(start, covered - half, 1),
        pltpu.roll(start, half, 1),
    )
    rotated = start * lanes_cosine + swapped * lanes_sine
    kv_ref[:, :covered] = jnp.where(lane < KEY_WIDTH, rotated, start).astype(jnp.bfloat16)
    kv_ref[:, covered:] = keyval[:, covered:].astype(jnp.bfloat16)


def project(hidden, gain, query_weight, keyval_weight, cosine, sine):
    rows, width = hidden.shape
    heads = query_weight.shape[0] // HEAD_SIZE
    half = HEAD_SIZE // 2
    return pl.pallas_call(
        project_kernel,
        grid=(rows // TILE,),
        in_specs=[
            pl.BlockSpec((TILE, width), lambda i: (i, 0)),
            pl.BlockSpec((1, width), lambda i: (0, 0)),
            pl.BlockSpec(query_weight.shape, lambda i: (0, 0)),
            pl.BlockSpec(keyval_weight.shape, lambda i: (0, 0)),
            pl.BlockSpec((half, TILE), lambda i: (0, i)),
            pl.BlockSpec((half, TILE), lambda i: (0, i)),
        ],
        out_specs=[
            pl.BlockSpec((heads, HEAD_SIZE, TILE), lambda i: (0, 0, i)),
            pl.BlockSpec((TILE, 2 * KEY_WIDTH), lambda i: (i, 0)),
        ],
        out_shape=[
            jax.ShapeDtypeStruct((heads, HEAD_SIZE, rows), jnp.bfloat16),
            jax.ShapeDtypeStruct((rows, 2 * KEY_WIDTH), jnp.bfloat16),
        ],
        compiler_params=pltpu.CompilerParams(vmem_limit_bytes=VMEM_BYTES),
    )(hidden, gain, query_weight, keyval_weight, cosine, sine)


def ship_kernel(block_rows, count, picks, sizes, prior_ref, fresh_ref, out_ref, sems):
    prior_blocks = PRIOR_SLOTS // block_rows

    def rows_of(block):
        return pl.ds(pl.multiple_of(block * block_rows, block_rows), block_rows)

    @pl.loop(0, count)
    def _(i):
        pick = picks[i]

        @pl.when(pick < prior_blocks)
        def _():
            pltpu.make_async_copy(prior_ref.at[rows_of(pick)], out_ref.at[i], sems.at[i]).start()

        @pl.when(pick >= prior_blocks)
        def _():
            pltpu.make_async_copy(
                fresh_ref.at[rows_of(pick - prior_blocks)], out_ref.at[i], sems.at[i]
            ).start()

    @pl.loop(0, count)
    def _(i):
        pick = picks[i]
        is_prior = pick < prior_blocks
        base = jnp.where(is_prior, pick, pick - prior_blocks) * block_rows
        live = jnp.where(is_prior, sizes[0], sizes[1])
        pltpu.make_async_copy(prior_ref.at[rows_of(0)], out_ref.at[i], sems.at[i]).wait()

        @pl.when(base + block_rows > live)
        def _():
            row = base + lax.broadcasted_iota(jnp.int32, (block_rows, 1), 0)
            out_ref[i] = jnp.where(row < live, out_ref[i], jnp.zeros((), jnp.bfloat16))


def pick_blocks(picks, sizes, prior, fresh, block_rows):
    count, width = picks.shape[0], prior.shape[1]
    return pl.pallas_call(
        functools.partial(ship_kernel, block_rows, count),
        in_specs=[
            pl.BlockSpec(memory_space=pltpu.SMEM),
            pl.BlockSpec(memory_space=pltpu.SMEM),
            pl.BlockSpec(memory_space=pl.ANY),
            pl.BlockSpec(memory_space=pl.ANY),
        ],
        out_specs=pl.BlockSpec(memory_space=pltpu.VMEM),
        out_shape=jax.ShapeDtypeStruct((count, block_rows, width), jnp.bfloat16),
        scratch_shapes=[pltpu.SemaphoreType.DMA((count,))],
        compiler_params=pltpu.CompilerParams(vmem_limit_bytes=VMEM_BYTES),
    )(picks, sizes, prior, fresh)


def attention_kernel(
    heads, sizes, q_ref, prior_ref, fresh_ref, out_ref, staged, keys, values, q_pair, top, acc, sems
):
    cached, fresh, first_kv = sizes[0], sizes[1], sizes[2]
    split = sizes[3]
    tiles = (fresh + TILE - 1) // TILE
    prior_live = (cached + KEYS - 1) // KEYS
    prior_whole = cached // KEYS
    remainder = cached - prior_whole * KEYS

    def fetch(block):
        rows = pl.ds(pl.multiple_of(block * KEYS, KEYS), KEYS)
        return pltpu.make_async_copy(prior_ref.at[rows], staged.at[rows], sems.at[block])

    @pl.loop(0, prior_live)
    def _(block):
        fetch(block).start()

    key_start = first_kv * HEAD_SIZE
    row_in = lax.broadcasted_iota(jnp.int32, (2 * KEY_WIDTH, PAIR), 0)
    lane_in = lax.broadcasted_iota(jnp.int32, (2 * KEY_WIDTH, PAIR), 1)
    choose_keys = (row_in == lane_in + key_start).astype(jnp.float32).astype(jnp.bfloat16)
    row_out = lax.broadcasted_iota(jnp.int32, (PAIR, 2 * KEY_WIDTH), 0)
    lane_out = lax.broadcasted_iota(jnp.int32, (PAIR, 2 * KEY_WIDTH), 1)
    choose_values = (
        (lane_out == row_out + key_start + KEY_WIDTH).astype(jnp.float32).astype(jnp.bfloat16)
    )

    def unpack(rows, at, count):
        keys[pl.ds(at, count), :] = jnp.dot(
            rows, choose_keys, preferred_element_type=jnp.float32
        ).astype(jnp.bfloat16)
        turned = lax.dot_general(
            choose_values, rows, (((1,), (1,)), ((), ())), preferred_element_type=jnp.float32
        ).astype(jnp.bfloat16)
        ones = jnp.ones((VALUE_ROWS - HEAD_SIZE, count), jnp.bfloat16)
        for half in range(2):
            values[half, :HEAD_SIZE, pl.ds(at, count)] = turned[
                half * HEAD_SIZE : (half + 1) * HEAD_SIZE
            ]
            values[half, HEAD_SIZE:, pl.ds(at, count)] = ones

    @pl.loop(0, tiles)
    def _(tile):
        rows = pl.ds(pl.multiple_of(tile * TILE, TILE), TILE)
        unpack(fresh_ref[rows, :], pl.multiple_of(PRIOR_SLOTS + tile * TILE, TILE), TILE)

    @pl.loop(0, prior_live)
    def _(block):
        fetch(block).wait()
        at = pl.multiple_of(block * KEYS, KEYS)
        unpack(staged[pl.ds(at, KEYS), :], at, KEYS)

    out_ref[...] = jnp.zeros_like(out_ref)

    def step(at, count, allowed):
        key_block = keys[pl.ds(at, count), :]

        def score(head):
            return jnp.dot(key_block, q_pair[head], preferred_element_type=jnp.float32)

        ahead = score(0)
        for head in range(heads):
            scores = ahead
            if head + 1 < heads:
                ahead = score(head + 1)
            if allowed is not None:
                scores = jnp.where(allowed, scores, -1e30)
            old = top[head]
            new = jnp.maximum(old, jnp.max(scores, axis=0, keepdims=True))
            top[head] = new
            chances = jnp.exp2(scores - new).astype(jnp.bfloat16)
            group = jnp.where(head < split, 0, 1)
            acc[head] = acc[head] * jnp.exp2(old - new) + jnp.dot(
                values[group, :, pl.ds(at, count)], chances, preferred_element_type=jnp.float32
            )

    @pl.loop(0, tiles)
    def _(tile):
        columns = pl.ds(pl.multiple_of(tile * TILE, TILE), TILE)
        for head in range(heads):
            query = q_ref[head, :, columns]
            none = jnp.zeros_like(query)
            lower = head < split
            q_pair[head, :HEAD_SIZE] = jnp.where(lower, query, none)
            q_pair[head, HEAD_SIZE:] = jnp.where(lower, none, query)
        top[...] = jnp.full_like(top, -1e30)
        acc[...] = jnp.zeros_like(acc)

        @pl.loop(0, prior_whole)
        def _(block):
            step(pl.multiple_of(block * KEYS, KEYS), KEYS, None)

        @pl.when(remainder > 0)
        def _():
            index = lax.broadcasted_iota(jnp.int32, (KEYS, TILE), 0)
            step(pl.multiple_of(prior_whole * KEYS, KEYS), KEYS, index < remainder)

        @pl.loop(0, tile)
        def _(block):
            step(pl.multiple_of(PRIOR_SLOTS + block * TILE, TILE), TILE, None)

        index = lax.broadcasted_iota(jnp.int32, (TILE, TILE), 0)
        slot = lax.broadcasted_iota(jnp.int32, (TILE, TILE), 1)
        step(pl.multiple_of(PRIOR_SLOTS + tile * TILE, TILE), TILE, index <= slot)
        for head in range(heads):
            total = acc[head]
            out_ref[tile, head * HEAD_SIZE : (head + 1) * HEAD_SIZE, :] = (
                total[:HEAD_SIZE] / total[HEAD_SIZE : HEAD_SIZE + 1]
            ).astype(jnp.bfloat16)


def attention(sizes, queries, prior, fresh_rows):
    heads = queries.shape[0]
    tiles = NEW_TOKEN_SLOTS // TILE
    context = PRIOR_SLOTS + NEW_TOKEN_SLOTS
    return pl.pallas_call(
        functools.partial(attention_kernel, heads),
        in_specs=[
            pl.BlockSpec(memory_space=pltpu.SMEM),
            pl.BlockSpec(memory_space=pltpu.VMEM),
            pl.BlockSpec(memory_space=pl.ANY),
            pl.BlockSpec(memory_space=pltpu.VMEM),
        ],
        out_specs=pl.BlockSpec(memory_space=pltpu.VMEM),
        out_shape=jax.ShapeDtypeStruct((tiles, heads * HEAD_SIZE, TILE), jnp.bfloat16),
        scratch_shapes=[
            pltpu.VMEM((PRIOR_SLOTS, 2 * KEY_WIDTH), jnp.bfloat16),
            pltpu.VMEM((context, PAIR), jnp.bfloat16),
            pltpu.VMEM((2, VALUE_ROWS, context), jnp.bfloat16),
            pltpu.VMEM((heads, PAIR, TILE), jnp.bfloat16),
            pltpu.VMEM((heads, 1, TILE), jnp.float32),
            pltpu.VMEM((heads, VALUE_ROWS, TILE), jnp.float32),
            pltpu.SemaphoreType.DMA((PRIOR_SLOTS // KEYS,)),
        ],
        compiler_params=pltpu.CompilerParams(vmem_limit_bytes=VMEM_BYTES),
        cost_estimate=pl.CostEstimate(
            flops=4 * NEW_TOKEN_SLOTS * heads * context * PAIR,
            bytes_accessed=2 * context * 2 * KEY_WIDTH,
            transcendentals=NEW_TOKEN_SLOTS * heads * context,
        ),
    )(sizes, queries, prior, fresh_rows)


def after_kernel(value_ref, other_ref, out_ref):
    del value_ref, other_ref, out_ref


def after(value, other):
    return pl.pallas_call(
        after_kernel,
        in_specs=[pl.BlockSpec(memory_space=pl.ANY)] * 2,
        out_specs=pl.BlockSpec(memory_space=pl.ANY),
        out_shape=jax.ShapeDtypeStruct(value.shape, value.dtype),
        input_output_aliases={0: 0},
    )(value, other)


def shards(
    hidden_in,
    norm_gain,
    w_query,
    key_value_weight,
    w_out,
    prior_cache,
    cache_len,
    group_len,
    page_map,
):
    rank = lax.axis_index("tp")
    tp_count = lax.axis_size("tp")
    req_count = lax.axis_size("req")
    span = hidden_in.shape[0] // tp_count
    heads = w_query.shape[1] // HEAD_SIZE
    blocks = page_map.shape[1]
    block_rows = (PRIOR_SLOTS + NEW_TOKEN_SLOTS) // blocks
    cached, fresh = cache_len[0], group_len[0]

    positions = cached + jnp.arange(NEW_TOKEN_SLOTS, dtype=jnp.int32)
    half = HEAD_SIZE // 2
    frequency = 10000.0 ** (-(jnp.arange(half, dtype=jnp.float32) * 2.0 / HEAD_SIZE))
    angles = frequency[:, None] * positions.astype(jnp.float32)[None, :]
    queries, fresh_rows = project(
        hidden_in, norm_gain[None], w_query.T, key_value_weight, jnp.cos(angles), jnp.sin(angles)
    )

    targets = jnp.arange(req_count, dtype=jnp.int32) * tp_count + rank
    picks = jnp.sum(
        jnp.where(
            page_map[0][None, :] == targets[:, None],
            jnp.arange(blocks, dtype=jnp.int32)[None, :],
            0,
        ),
        axis=1,
    ).astype(jnp.int32)
    first_head = rank * heads
    group = QUERY_HEAD_COUNT // KEY_VALUE_HEADS
    first_kv = first_head // group
    split = (first_kv + 1) * group - first_head
    sizes = jnp.stack([cached, fresh, first_kv, split]).astype(jnp.int32)

    shipment = pick_blocks(picks, sizes, prior_cache[0], fresh_rows, block_rows)
    decode_kv = lax.all_to_all(shipment, "req", split_axis=0, concat_axis=0, tiled=True)[None]

    attended = attention(sizes, queries, prior_cache[0], fresh_rows)
    attended = after(attended, decode_kv)
    gathered = lax.all_to_all(attended, "tp", split_axis=0, concat_axis=0, tiled=True)
    mixed = lax.dot_general(
        gathered.reshape(QUERY_HEAD_COUNT * HEAD_SIZE, span),
        w_out,
        (((0,), (0,)), ((), ())),
        preferred_element_type=jnp.float32,
    )
    live = rank * span + jnp.arange(span, dtype=jnp.int32) < fresh
    own = lax.dynamic_slice_in_dim(hidden_in, rank * span, span, 0).astype(jnp.float32)
    hidden_out = jnp.where(live[:, None], own + mixed, 0.0).astype(jnp.bfloat16)
    return (hidden_out, decode_kv)


def solution(mesh):
    placed = (
        P("req", None),
        P(),
        P(None, "tp"),
        P(),
        P(),
        P("req", None, None),
        P("req"),
        P("req"),
        P("req", None),
    )
    return jax.shard_map(
        shards,
        mesh=mesh,
        in_specs=placed,
        out_specs=(P(("req", "tp"), None), P(("req", "tp"), None, None, None)),
        check_vma=False,
    )
```

```python
import functools
import math

import jax
import jax.numpy as jnp
from jax import lax
from jax.experimental import pallas as pl
from jax.experimental.pallas import tpu as pltpu
from jax.sharding import PartitionSpec as P

QUERY_HEAD_COUNT = 20
KEY_VALUE_HEADS = 5
HEAD_SIZE = 64
NEW_TOKEN_SLOTS = 1024
PRIOR_SLOTS = 7168
KEY_WIDTH = KEY_VALUE_HEADS * HEAD_SIZE
KEYS = 512
TILE = 256
PAIR = 2 * HEAD_SIZE
VALUE_ROWS = 80
LANES = 128
QUERY_SCALE = HEAD_SIZE ** (-0.5) * math.log2(math.e)
VMEM_BYTES = 50 * 1024 * 1024


def project_kernel(
    hidden_ref, gain_ref, query_weight_ref, keyval_weight_ref, cosine_ref, sine_ref, q_ref, kv_ref
):
    half = HEAD_SIZE // 2
    hidden = hidden_ref[...].astype(jnp.float32)
    normed = (
        hidden
        * lax.rsqrt(jnp.mean(hidden * hidden, axis=-1, keepdims=True) + 1e-05)
        * gain_ref[...].astype(jnp.float32)
    ).astype(jnp.bfloat16)
    cosine, sine = cosine_ref[...], sine_ref[...]

    turned = lax.dot_general(
        query_weight_ref[...], normed, (((1,), (1,)), ((), ())), preferred_element_type=jnp.float32
    )
    for head in range(q_ref.shape[0]):
        first = turned[head * HEAD_SIZE : head * HEAD_SIZE + half]
        second = turned[head * HEAD_SIZE + half : (head + 1) * HEAD_SIZE]
        q_ref[head, :half] = ((first * cosine - second * sine) * QUERY_SCALE).astype(jnp.bfloat16)
        q_ref[head, half:] = ((second * cosine + first * sine) * QUERY_SCALE).astype(jnp.bfloat16)

    keyval = jnp.dot(normed, keyval_weight_ref[...], preferred_element_type=jnp.float32)
    covered = (KEY_WIDTH + LANES - 1) // LANES * LANES
    repeat = LANES // half
    lanes_cosine = jnp.concatenate([jnp.concatenate([cosine] * repeat, axis=0).T] * (covered // LANES), axis=1)
    lanes_sine = jnp.concatenate([jnp.concatenate([sine] * repeat, axis=0).T] * (covered // LANES), axis=1)
    start = keyval[:, :covered]
    lane = lax.broadcasted_iota(jnp.int32, start.shape, 1)
    swapped = jnp.where(
        lane % HEAD_SIZE < half,
        -pltpu.roll(start, covered - half, 1),
        pltpu.roll(start, half, 1),
    )
    rotated = start * lanes_cosine + swapped * lanes_sine
    kv_ref[:, :covered] = jnp.where(lane < KEY_WIDTH, rotated, start).astype(jnp.bfloat16)
    kv_ref[:, covered:] = keyval[:, covered:].astype(jnp.bfloat16)


def project(hidden, gain, query_weight, keyval_weight, cosine, sine):
    rows, width = hidden.shape
    heads = query_weight.shape[0] // HEAD_SIZE
    half = HEAD_SIZE // 2
    return pl.pallas_call(
        project_kernel,
        grid=(rows // TILE,),
        in_specs=[
            pl.BlockSpec((TILE, width), lambda i: (i, 0)),
            pl.BlockSpec((1, width), lambda i: (0, 0)),
            pl.BlockSpec(query_weight.shape, lambda i: (0, 0)),
            pl.BlockSpec(keyval_weight.shape, lambda i: (0, 0)),
            pl.BlockSpec((half, TILE), lambda i: (0, i)),
            pl.BlockSpec((half, TILE), lambda i: (0, i)),
        ],
        out_specs=[
            pl.BlockSpec((heads, HEAD_SIZE, TILE), lambda i: (0, 0, i)),
            pl.BlockSpec((TILE, 2 * KEY_WIDTH), lambda i: (i, 0)),
        ],
        out_shape=[
            jax.ShapeDtypeStruct((heads, HEAD_SIZE, rows), jnp.bfloat16),
            jax.ShapeDtypeStruct((rows, 2 * KEY_WIDTH), jnp.bfloat16),
        ],
        compiler_params=pltpu.CompilerParams(vmem_limit_bytes=VMEM_BYTES),
    )(hidden, gain, query_weight, keyval_weight, cosine, sine)


def ship_kernel(block_rows, count, picks, sizes, prior_ref, fresh_ref, out_ref, sems):
    prior_blocks = PRIOR_SLOTS // block_rows

    def rows_of(block):
        return pl.ds(pl.multiple_of(block * block_rows, block_rows), block_rows)

    @pl.loop(0, count)
    def _(i):
        pick = picks[i]

        @pl.when(pick < prior_blocks)
        def _():
            pltpu.make_async_copy(prior_ref.at[rows_of(pick)], out_ref.at[i], sems.at[i]).start()

        @pl.when(pick >= prior_blocks)
        def _():
            pltpu.make_async_copy(
                fresh_ref.at[rows_of(pick - prior_blocks)], out_ref.at[i], sems.at[i]
            ).start()

    @pl.loop(0, count)
    def _(i):
        pick = picks[i]
        is_prior = pick < prior_blocks
        base = jnp.where(is_prior, pick, pick - prior_blocks) * block_rows
        live = jnp.where(is_prior, sizes[0], sizes[1])
        pltpu.make_async_copy(prior_ref.at[rows_of(0)], out_ref.at[i], sems.at[i]).wait()

        @pl.when(base + block_rows > live)
        def _():
            row = base + lax.broadcasted_iota(jnp.int32, (block_rows, 1), 0)
            out_ref[i] = jnp.where(row < live, out_ref[i], jnp.zeros((), jnp.bfloat16))


def pick_blocks(picks, sizes, prior, fresh, block_rows):
    count, width = picks.shape[0], prior.shape[1]
    return pl.pallas_call(
        functools.partial(ship_kernel, block_rows, count),
        in_specs=[
            pl.BlockSpec(memory_space=pltpu.SMEM),
            pl.BlockSpec(memory_space=pltpu.SMEM),
            pl.BlockSpec(memory_space=pl.ANY),
            pl.BlockSpec(memory_space=pl.ANY),
        ],
        out_specs=pl.BlockSpec(memory_space=pltpu.VMEM),
        out_shape=jax.ShapeDtypeStruct((count, block_rows, width), jnp.bfloat16),
        scratch_shapes=[pltpu.SemaphoreType.DMA((count,))],
        compiler_params=pltpu.CompilerParams(vmem_limit_bytes=VMEM_BYTES),
    )(picks, sizes, prior, fresh)


def attention_kernel(
    heads, sizes, q_ref, prior_ref, fresh_ref, out_ref, staged, keys, values, q_pair, top, acc, sems
):
    cached, fresh, first_kv = sizes[0], sizes[1], sizes[2]
    split = sizes[3]
    tiles = (fresh + TILE - 1) // TILE
    prior_live = (cached + KEYS - 1) // KEYS
    prior_whole = cached // KEYS
    remainder = cached - prior_whole * KEYS

    def fetch(block):
        rows = pl.ds(pl.multiple_of(block * KEYS, KEYS), KEYS)
        return pltpu.make_async_copy(prior_ref.at[rows], staged.at[rows], sems.at[block])

    @pl.loop(0, prior_live)
    def _(block):
        fetch(block).start()

    key_start = first_kv * HEAD_SIZE
    row_in = lax.broadcasted_iota(jnp.int32, (2 * KEY_WIDTH, PAIR), 0)
    lane_in = lax.broadcasted_iota(jnp.int32, (2 * KEY_WIDTH, PAIR), 1)
    choose_keys = (row_in == lane_in + key_start).astype(jnp.float32).astype(jnp.bfloat16)
    row_out = lax.broadcasted_iota(jnp.int32, (PAIR, 2 * KEY_WIDTH), 0)
    lane_out = lax.broadcasted_iota(jnp.int32, (PAIR, 2 * KEY_WIDTH), 1)
    choose_values = (
        (lane_out == row_out + key_start + KEY_WIDTH).astype(jnp.float32).astype(jnp.bfloat16)
    )

    def unpack(rows, at, count):
        keys[pl.ds(at, count), :] = jnp.dot(
            rows, choose_keys, preferred_element_type=jnp.float32
        ).astype(jnp.bfloat16)
        turned = lax.dot_general(
            choose_values, rows, (((1,), (1,)), ((), ())), preferred_element_type=jnp.float32
        ).astype(jnp.bfloat16)
        ones = jnp.ones((VALUE_ROWS - HEAD_SIZE, count), jnp.bfloat16)
        for half in range(2):
            values[half, :HEAD_SIZE, pl.ds(at, count)] = turned[
                half * HEAD_SIZE : (half + 1) * HEAD_SIZE
            ]
            values[half, HEAD_SIZE:, pl.ds(at, count)] = ones

    @pl.loop(0, tiles)
    def _(tile):
        rows = pl.ds(pl.multiple_of(tile * TILE, TILE), TILE)
        unpack(fresh_ref[rows, :], pl.multiple_of(PRIOR_SLOTS + tile * TILE, TILE), TILE)

    @pl.loop(0, prior_live)
    def _(block):
        fetch(block).wait()
        at = pl.multiple_of(block * KEYS, KEYS)
        unpack(staged[pl.ds(at, KEYS), :], at, KEYS)

    out_ref[...] = jnp.zeros_like(out_ref)

    def step(starts, count, allowed):
        items = [(at, head) for at in starts for head in range(heads)]

        def score(at, head):
            return jnp.dot(
                keys[pl.ds(at, count), :], q_pair[head], preferred_element_type=jnp.float32
            )

        def gather_values(at, head, rescale, chances):
            group = jnp.where(head < split, 0, 1)
            acc[head] = acc[head] * rescale + jnp.dot(
                values[group, :, pl.ds(at, count)], chances, preferred_element_type=jnp.float32
            )

        ahead = score(*items[0])
        pending = None
        for index, (at, head) in enumerate(items):
            scores = ahead
            if index + 1 < len(items):
                ahead = score(*items[index + 1])
            if allowed is not None:
                scores = jnp.where(allowed, scores, -1e30)
            old = top[head]
            new = jnp.maximum(old, jnp.max(scores, axis=0, keepdims=True))
            top[head] = new
            chances = jnp.exp2((scores - new).astype(jnp.bfloat16))
            if pending is not None:
                gather_values(*pending)
            pending = (at, head, jnp.exp2(old - new), chances)
        gather_values(*pending)

    @pl.loop(0, tiles)
    def _(tile):
        columns = pl.ds(pl.multiple_of(tile * TILE, TILE), TILE)
        for head in range(heads):
            query = q_ref[head, :, columns]
            none = jnp.zeros_like(query)
            lower = head < split
            q_pair[head, :HEAD_SIZE] = jnp.where(lower, query, none)
            q_pair[head, HEAD_SIZE:] = jnp.where(lower, none, query)
        top[...] = jnp.full_like(top, -1e30)
        acc[...] = jnp.zeros_like(acc)

        @pl.loop(0, prior_whole // 2)
        def _(pair):
            at = pl.multiple_of(pair * (2 * KEYS), 2 * KEYS)
            step([at, pl.multiple_of(at + KEYS, KEYS)], KEYS, None)

        @pl.when(prior_whole % 2 == 1)
        def _():
            step([pl.multiple_of((prior_whole - 1) * KEYS, KEYS)], KEYS, None)

        @pl.when(remainder > 0)
        def _():
            index = lax.broadcasted_iota(jnp.int32, (KEYS, TILE), 0)
            step([pl.multiple_of(prior_whole * KEYS, KEYS)], KEYS, index < remainder)

        @pl.loop(0, tile)
        def _(block):
            step([pl.multiple_of(PRIOR_SLOTS + block * TILE, TILE)], TILE, None)

        index = lax.broadcasted_iota(jnp.int32, (TILE, TILE), 0)
        slot = lax.broadcasted_iota(jnp.int32, (TILE, TILE), 1)
        step([pl.multiple_of(PRIOR_SLOTS + tile * TILE, TILE)], TILE, index <= slot)
        for head in range(heads):
            total = acc[head]
            out_ref[tile, head * HEAD_SIZE : (head + 1) * HEAD_SIZE, :] = (
                total[:HEAD_SIZE] / total[HEAD_SIZE : HEAD_SIZE + 1]
            ).astype(jnp.bfloat16)


def attention(sizes, queries, prior, fresh_rows):
    heads = queries.shape[0]
    tiles = NEW_TOKEN_SLOTS // TILE
    context = PRIOR_SLOTS + NEW_TOKEN_SLOTS
    return pl.pallas_call(
        functools.partial(attention_kernel, heads),
        in_specs=[
            pl.BlockSpec(memory_space=pltpu.SMEM),
            pl.BlockSpec(memory_space=pltpu.VMEM),
            pl.BlockSpec(memory_space=pl.ANY),
            pl.BlockSpec(memory_space=pltpu.VMEM),
        ],
        out_specs=pl.BlockSpec(memory_space=pltpu.VMEM),
        out_shape=jax.ShapeDtypeStruct((tiles, heads * HEAD_SIZE, TILE), jnp.bfloat16),
        scratch_shapes=[
            pltpu.VMEM((PRIOR_SLOTS, 2 * KEY_WIDTH), jnp.bfloat16),
            pltpu.VMEM((context, PAIR), jnp.bfloat16),
            pltpu.VMEM((2, VALUE_ROWS, context), jnp.bfloat16),
            pltpu.VMEM((heads, PAIR, TILE), jnp.bfloat16),
            pltpu.VMEM((heads, 1, TILE), jnp.float32),
            pltpu.VMEM((heads, VALUE_ROWS, TILE), jnp.float32),
            pltpu.SemaphoreType.DMA((PRIOR_SLOTS // KEYS,)),
        ],
        compiler_params=pltpu.CompilerParams(vmem_limit_bytes=VMEM_BYTES),
        cost_estimate=pl.CostEstimate(
            flops=4 * NEW_TOKEN_SLOTS * heads * context * PAIR,
            bytes_accessed=2 * context * 2 * KEY_WIDTH,
            transcendentals=NEW_TOKEN_SLOTS * heads * context,
        ),
    )(sizes, queries, prior, fresh_rows)


def after_kernel(value_ref, other_ref, out_ref):
    del value_ref, other_ref, out_ref


def after(value, other):
    return pl.pallas_call(
        after_kernel,
        in_specs=[pl.BlockSpec(memory_space=pl.ANY)] * 2,
        out_specs=pl.BlockSpec(memory_space=pl.ANY),
        out_shape=jax.ShapeDtypeStruct(value.shape, value.dtype),
        input_output_aliases={0: 0},
    )(value, other)


def shards(
    hidden_in,
    norm_gain,
    w_query,
    key_value_weight,
    w_out,
    prior_cache,
    cache_len,
    group_len,
    page_map,
):
    rank = lax.axis_index("tp")
    tp_count = lax.axis_size("tp")
    req_count = lax.axis_size("req")
    span = hidden_in.shape[0] // tp_count
    heads = w_query.shape[1] // HEAD_SIZE
    blocks = page_map.shape[1]
    block_rows = (PRIOR_SLOTS + NEW_TOKEN_SLOTS) // blocks
    cached, fresh = cache_len[0], group_len[0]

    positions = cached + jnp.arange(NEW_TOKEN_SLOTS, dtype=jnp.int32)
    half = HEAD_SIZE // 2
    frequency = 10000.0 ** (-(jnp.arange(half, dtype=jnp.float32) * 2.0 / HEAD_SIZE))
    angles = frequency[:, None] * positions.astype(jnp.float32)[None, :]
    queries, fresh_rows = project(
        hidden_in, norm_gain[None], w_query.T, key_value_weight, jnp.cos(angles), jnp.sin(angles)
    )

    targets = jnp.arange(req_count, dtype=jnp.int32) * tp_count + rank
    picks = jnp.sum(
        jnp.where(
            page_map[0][None, :] == targets[:, None],
            jnp.arange(blocks, dtype=jnp.int32)[None, :],
            0,
        ),
        axis=1,
    ).astype(jnp.int32)
    first_head = rank * heads
    group = QUERY_HEAD_COUNT // KEY_VALUE_HEADS
    first_kv = first_head // group
    split = (first_kv + 1) * group - first_head
    sizes = jnp.stack([cached, fresh, first_kv, split]).astype(jnp.int32)

    shipment = pick_blocks(picks, sizes, prior_cache[0], fresh_rows, block_rows)
    decode_kv = lax.all_to_all(shipment, "req", split_axis=0, concat_axis=0, tiled=True)[None]

    attended = attention(sizes, queries, prior_cache[0], fresh_rows)
    attended = after(attended, decode_kv)
    gathered = lax.all_to_all(attended, "tp", split_axis=0, concat_axis=0, tiled=True)
    mixed = lax.dot_general(
        gathered.reshape(QUERY_HEAD_COUNT * HEAD_SIZE, span),
        w_out,
        (((0,), (0,)), ((), ())),
        preferred_element_type=jnp.float32,
    )
    live = rank * span + jnp.arange(span, dtype=jnp.int32) < fresh
    own = lax.dynamic_slice_in_dim(hidden_in, rank * span, span, 0).astype(jnp.float32)
    hidden_out = jnp.where(live[:, None], own + mixed, 0.0).astype(jnp.bfloat16)
    return (hidden_out, decode_kv)


def solution(mesh):
    placed = (
        P("req", None),
        P(),
        P(None, "tp"),
        P(),
        P(),
        P("req", None, None),
        P("req"),
        P("req"),
        P("req", None),
    )
    return jax.shard_map(
        shards,
        mesh=mesh,
        in_specs=placed,
        out_specs=(P(("req", "tp"), None), P(("req", "tp"), None, None, None)),
        check_vma=False,
    )
```

```python
import functools
import math

import jax
import jax.numpy as jnp
from jax import lax
from jax.experimental import pallas as pl
from jax.experimental.pallas import tpu as pltpu
from jax.sharding import PartitionSpec as P

QUERY_HEAD_COUNT = 20
KEY_VALUE_HEADS = 5
HEAD_SIZE = 64
NEW_TOKEN_SLOTS = 1024
PRIOR_SLOTS = 7168
KEY_WIDTH = KEY_VALUE_HEADS * HEAD_SIZE
KEYS = 512
TILE = 256
PAIR = 2 * HEAD_SIZE
VALUE_ROWS = 80
LANES = 128
QUERY_SCALE = HEAD_SIZE ** (-0.5) * math.log2(math.e)
VMEM_BYTES = 50 * 1024 * 1024


def project_kernel(
    hidden_ref, gain_ref, query_weight_ref, keyval_weight_ref, cosine_ref, sine_ref, q_ref, kv_ref
):
    half = HEAD_SIZE // 2
    hidden = hidden_ref[...].astype(jnp.float32)
    normed = (
        hidden
        * lax.rsqrt(jnp.mean(hidden * hidden, axis=-1, keepdims=True) + 1e-05)
        * gain_ref[...].astype(jnp.float32)
    ).astype(jnp.bfloat16)
    cosine, sine = cosine_ref[...], sine_ref[...]

    turned = lax.dot_general(
        query_weight_ref[...], normed, (((1,), (1,)), ((), ())), preferred_element_type=jnp.float32
    )
    for head in range(q_ref.shape[0]):
        first = turned[head * HEAD_SIZE : head * HEAD_SIZE + half]
        second = turned[head * HEAD_SIZE + half : (head + 1) * HEAD_SIZE]
        q_ref[head, :half] = ((first * cosine - second * sine) * QUERY_SCALE).astype(jnp.bfloat16)
        q_ref[head, half:] = ((second * cosine + first * sine) * QUERY_SCALE).astype(jnp.bfloat16)

    keyval = jnp.dot(normed, keyval_weight_ref[...], preferred_element_type=jnp.float32)
    covered = (KEY_WIDTH + LANES - 1) // LANES * LANES
    repeat = LANES // half
    lanes_cosine = jnp.concatenate([jnp.concatenate([cosine] * repeat, axis=0).T] * (covered // LANES), axis=1)
    lanes_sine = jnp.concatenate([jnp.concatenate([sine] * repeat, axis=0).T] * (covered // LANES), axis=1)
    start = keyval[:, :covered]
    lane = lax.broadcasted_iota(jnp.int32, start.shape, 1)
    swapped = jnp.where(
        lane % HEAD_SIZE < half,
        -pltpu.roll(start, covered - half, 1),
        pltpu.roll(start, half, 1),
    )
    rotated = start * lanes_cosine + swapped * lanes_sine
    kv_ref[:, :covered] = jnp.where(lane < KEY_WIDTH, rotated, start).astype(jnp.bfloat16)
    kv_ref[:, covered:] = keyval[:, covered:].astype(jnp.bfloat16)


def project(hidden, gain, query_weight, keyval_weight, cosine, sine):
    rows, width = hidden.shape
    heads = query_weight.shape[0] // HEAD_SIZE
    half = HEAD_SIZE // 2
    return pl.pallas_call(
        project_kernel,
        grid=(rows // TILE,),
        in_specs=[
            pl.BlockSpec((TILE, width), lambda i: (i, 0)),
            pl.BlockSpec((1, width), lambda i: (0, 0)),
            pl.BlockSpec(query_weight.shape, lambda i: (0, 0)),
            pl.BlockSpec(keyval_weight.shape, lambda i: (0, 0)),
            pl.BlockSpec((half, TILE), lambda i: (0, i)),
            pl.BlockSpec((half, TILE), lambda i: (0, i)),
        ],
        out_specs=[
            pl.BlockSpec((heads, HEAD_SIZE, TILE), lambda i: (0, 0, i)),
            pl.BlockSpec((TILE, 2 * KEY_WIDTH), lambda i: (i, 0)),
        ],
        out_shape=[
            jax.ShapeDtypeStruct((heads, HEAD_SIZE, rows), jnp.bfloat16),
            jax.ShapeDtypeStruct((rows, 2 * KEY_WIDTH), jnp.bfloat16),
        ],
        compiler_params=pltpu.CompilerParams(vmem_limit_bytes=VMEM_BYTES),
    )(hidden, gain, query_weight, keyval_weight, cosine, sine)


def ship_kernel(block_rows, count, picks, sizes, prior_ref, fresh_ref, out_ref, sems):
    prior_blocks = PRIOR_SLOTS // block_rows

    def rows_of(block):
        return pl.ds(pl.multiple_of(block * block_rows, block_rows), block_rows)

    @pl.loop(0, count)
    def _(i):
        pick = picks[i]

        @pl.when(pick < prior_blocks)
        def _():
            pltpu.make_async_copy(prior_ref.at[rows_of(pick)], out_ref.at[i], sems.at[i]).start()

        @pl.when(pick >= prior_blocks)
        def _():
            pltpu.make_async_copy(
                fresh_ref.at[rows_of(pick - prior_blocks)], out_ref.at[i], sems.at[i]
            ).start()

    @pl.loop(0, count)
    def _(i):
        pick = picks[i]
        is_prior = pick < prior_blocks
        base = jnp.where(is_prior, pick, pick - prior_blocks) * block_rows
        live = jnp.where(is_prior, sizes[0], sizes[1])
        pltpu.make_async_copy(prior_ref.at[rows_of(0)], out_ref.at[i], sems.at[i]).wait()

        @pl.when(base + block_rows > live)
        def _():
            row = base + lax.broadcasted_iota(jnp.int32, (block_rows, 1), 0)
            out_ref[i] = jnp.where(row < live, out_ref[i], jnp.zeros((), jnp.bfloat16))


def pick_blocks(picks, sizes, prior, fresh, block_rows):
    count, width = picks.shape[0], prior.shape[1]
    return pl.pallas_call(
        functools.partial(ship_kernel, block_rows, count),
        in_specs=[
            pl.BlockSpec(memory_space=pltpu.SMEM),
            pl.BlockSpec(memory_space=pltpu.SMEM),
            pl.BlockSpec(memory_space=pl.ANY),
            pl.BlockSpec(memory_space=pl.ANY),
        ],
        out_specs=pl.BlockSpec(memory_space=pltpu.VMEM),
        out_shape=jax.ShapeDtypeStruct((count, block_rows, width), jnp.bfloat16),
        scratch_shapes=[pltpu.SemaphoreType.DMA((count,))],
        compiler_params=pltpu.CompilerParams(vmem_limit_bytes=VMEM_BYTES),
    )(picks, sizes, prior, fresh)


def attention_kernel(
    heads, sizes, q_ref, prior_ref, fresh_ref, out_ref, staged, keys, values, q_pair, top, acc, sems
):
    cached, fresh, first_kv = sizes[0], sizes[1], sizes[2]
    split = sizes[3]
    tiles = (fresh + TILE - 1) // TILE
    prior_live = (cached + KEYS - 1) // KEYS
    prior_whole = cached // KEYS
    remainder = cached - prior_whole * KEYS

    def fetch(block):
        rows = pl.ds(pl.multiple_of(block * KEYS, KEYS), KEYS)
        return pltpu.make_async_copy(prior_ref.at[rows], staged.at[rows], sems.at[block])

    @pl.loop(0, prior_live)
    def _(block):
        fetch(block).start()

    key_start = first_kv * HEAD_SIZE
    row_in = lax.broadcasted_iota(jnp.int32, (2 * KEY_WIDTH, PAIR), 0)
    lane_in = lax.broadcasted_iota(jnp.int32, (2 * KEY_WIDTH, PAIR), 1)
    choose_keys = (row_in == lane_in + key_start).astype(jnp.float32).astype(jnp.bfloat16)
    row_out = lax.broadcasted_iota(jnp.int32, (PAIR, 2 * KEY_WIDTH), 0)
    lane_out = lax.broadcasted_iota(jnp.int32, (PAIR, 2 * KEY_WIDTH), 1)
    choose_values = (
        (lane_out == row_out + key_start + KEY_WIDTH).astype(jnp.float32).astype(jnp.bfloat16)
    )

    def unpack(rows, at, count):
        keys[pl.ds(at, count), :] = jnp.dot(
            rows, choose_keys, preferred_element_type=jnp.float32
        ).astype(jnp.bfloat16)
        turned = lax.dot_general(
            choose_values, rows, (((1,), (1,)), ((), ())), preferred_element_type=jnp.float32
        ).astype(jnp.bfloat16)
        ones = jnp.ones((VALUE_ROWS - HEAD_SIZE, count), jnp.bfloat16)
        for half in range(2):
            values[half, :HEAD_SIZE, pl.ds(at, count)] = turned[
                half * HEAD_SIZE : (half + 1) * HEAD_SIZE
            ]
            values[half, HEAD_SIZE:, pl.ds(at, count)] = ones

    @pl.loop(0, tiles)
    def _(tile):
        rows = pl.ds(pl.multiple_of(tile * TILE, TILE), TILE)
        unpack(fresh_ref[rows, :], pl.multiple_of(PRIOR_SLOTS + tile * TILE, TILE), TILE)

    @pl.loop(0, prior_live)
    def _(block):
        fetch(block).wait()
        at = pl.multiple_of(block * KEYS, KEYS)
        unpack(staged[pl.ds(at, KEYS), :], at, KEYS)

    out_ref[...] = jnp.zeros_like(out_ref)

    def step(starts, count, allowed):
        items = [(at, head) for at in starts for head in range(heads)]

        def score(at, head):
            return jnp.dot(
                keys[pl.ds(at, count), :], q_pair[head], preferred_element_type=jnp.float32
            )

        def gather_values(at, head, rescale, chances):
            group = jnp.where(head < split, 0, 1)
            acc[head] = acc[head] * rescale + jnp.dot(
                values[group, :, pl.ds(at, count)], chances, preferred_element_type=jnp.float32
            )

        ahead = score(*items[0])
        pending = None
        for index, (at, head) in enumerate(items):
            scores = ahead
            if index + 1 < len(items):
                ahead = score(*items[index + 1])
            if allowed is not None:
                scores = jnp.where(allowed, scores, -1e30)
            old = top[head]
            new = jnp.maximum(old, jnp.max(scores, axis=0, keepdims=True))
            top[head] = new
            chances = jnp.exp2((scores - new).astype(jnp.bfloat16))
            if pending is not None:
                gather_values(*pending)
            pending = (at, head, jnp.exp2(old - new), chances)
        gather_values(*pending)

    @pl.loop(0, tiles)
    def _(tile):
        columns = pl.ds(pl.multiple_of(tile * TILE, TILE), TILE)
        for head in range(heads):
            query = q_ref[head, :, columns]
            none = jnp.zeros_like(query)
            lower = head < split
            q_pair[head, :HEAD_SIZE] = jnp.where(lower, query, none)
            q_pair[head, HEAD_SIZE:] = jnp.where(lower, none, query)
        top[...] = jnp.full_like(top, -1e30)
        acc[...] = jnp.zeros_like(acc)

        @pl.loop(0, prior_whole // 4)
        def _(quad):
            at = pl.multiple_of(quad * (4 * KEYS), 4 * KEYS)
            step([pl.multiple_of(at + part * KEYS, KEYS) for part in range(4)], KEYS, None)

        @pl.when(prior_whole % 4 >= 2)
        def _():
            at = pl.multiple_of((prior_whole // 4) * (4 * KEYS), KEYS)
            step([at, pl.multiple_of(at + KEYS, KEYS)], KEYS, None)

        @pl.when(prior_whole % 2 == 1)
        def _():
            step([pl.multiple_of((prior_whole - 1) * KEYS, KEYS)], KEYS, None)

        @pl.when(remainder > 0)
        def _():
            index = lax.broadcasted_iota(jnp.int32, (KEYS, TILE), 0)
            step([pl.multiple_of(prior_whole * KEYS, KEYS)], KEYS, index < remainder)

        @pl.loop(0, tile)
        def _(block):
            step([pl.multiple_of(PRIOR_SLOTS + block * TILE, TILE)], TILE, None)

        index = lax.broadcasted_iota(jnp.int32, (TILE, TILE), 0)
        slot = lax.broadcasted_iota(jnp.int32, (TILE, TILE), 1)
        step([pl.multiple_of(PRIOR_SLOTS + tile * TILE, TILE)], TILE, index <= slot)
        for head in range(heads):
            total = acc[head]
            out_ref[tile, head * HEAD_SIZE : (head + 1) * HEAD_SIZE, :] = (
                total[:HEAD_SIZE] / total[HEAD_SIZE : HEAD_SIZE + 1]
            ).astype(jnp.bfloat16)


def attention(sizes, queries, prior, fresh_rows):
    heads = queries.shape[0]
    tiles = NEW_TOKEN_SLOTS // TILE
    context = PRIOR_SLOTS + NEW_TOKEN_SLOTS
    return pl.pallas_call(
        functools.partial(attention_kernel, heads),
        in_specs=[
            pl.BlockSpec(memory_space=pltpu.SMEM),
            pl.BlockSpec(memory_space=pltpu.VMEM),
            pl.BlockSpec(memory_space=pl.ANY),
            pl.BlockSpec(memory_space=pltpu.VMEM),
        ],
        out_specs=pl.BlockSpec(memory_space=pltpu.VMEM),
        out_shape=jax.ShapeDtypeStruct((tiles, heads * HEAD_SIZE, TILE), jnp.bfloat16),
        scratch_shapes=[
            pltpu.VMEM((PRIOR_SLOTS, 2 * KEY_WIDTH), jnp.bfloat16),
            pltpu.VMEM((context, PAIR), jnp.bfloat16),
            pltpu.VMEM((2, VALUE_ROWS, context), jnp.bfloat16),
            pltpu.VMEM((heads, PAIR, TILE), jnp.bfloat16),
            pltpu.VMEM((heads, 1, TILE), jnp.float32),
            pltpu.VMEM((heads, VALUE_ROWS, TILE), jnp.float32),
            pltpu.SemaphoreType.DMA((PRIOR_SLOTS // KEYS,)),
        ],
        compiler_params=pltpu.CompilerParams(vmem_limit_bytes=VMEM_BYTES),
        cost_estimate=pl.CostEstimate(
            flops=4 * NEW_TOKEN_SLOTS * heads * context * PAIR,
            bytes_accessed=2 * context * 2 * KEY_WIDTH,
            transcendentals=NEW_TOKEN_SLOTS * heads * context,
        ),
    )(sizes, queries, prior, fresh_rows)


def after_kernel(value_ref, other_ref, out_ref, copied_ref, sem):
    del value_ref, out_ref
    copy = pltpu.make_async_copy(other_ref, copied_ref, sem)
    copy.start()
    copy.wait()


def after(value, other):
    return pl.pallas_call(
        after_kernel,
        in_specs=[pl.BlockSpec(memory_space=pl.ANY)] * 2,
        out_specs=[pl.BlockSpec(memory_space=pl.ANY)] * 2,
        out_shape=[
            jax.ShapeDtypeStruct(value.shape, value.dtype),
            jax.ShapeDtypeStruct(other.shape, other.dtype),
        ],
        input_output_aliases={0: 0},
        scratch_shapes=[pltpu.SemaphoreType.DMA],
    )(value, other)


def shards(
    hidden_in,
    norm_gain,
    w_query,
    key_value_weight,
    w_out,
    prior_cache,
    cache_len,
    group_len,
    page_map,
):
    rank = lax.axis_index("tp")
    tp_count = lax.axis_size("tp")
    req_count = lax.axis_size("req")
    span = hidden_in.shape[0] // tp_count
    heads = w_query.shape[1] // HEAD_SIZE
    blocks = page_map.shape[1]
    block_rows = (PRIOR_SLOTS + NEW_TOKEN_SLOTS) // blocks
    cached, fresh = cache_len[0], group_len[0]

    positions = cached + jnp.arange(NEW_TOKEN_SLOTS, dtype=jnp.int32)
    half = HEAD_SIZE // 2
    frequency = 10000.0 ** (-(jnp.arange(half, dtype=jnp.float32) * 2.0 / HEAD_SIZE))
    angles = frequency[:, None] * positions.astype(jnp.float32)[None, :]
    queries, fresh_rows = project(
        hidden_in, norm_gain[None], w_query.T, key_value_weight, jnp.cos(angles), jnp.sin(angles)
    )

    targets = jnp.arange(req_count, dtype=jnp.int32) * tp_count + rank
    picks = jnp.sum(
        jnp.where(
            page_map[0][None, :] == targets[:, None],
            jnp.arange(blocks, dtype=jnp.int32)[None, :],
            0,
        ),
        axis=1,
    ).astype(jnp.int32)
    first_head = rank * heads
    group = QUERY_HEAD_COUNT // KEY_VALUE_HEADS
    first_kv = first_head // group
    split = (first_kv + 1) * group - first_head
    sizes = jnp.stack([cached, fresh, first_kv, split]).astype(jnp.int32)

    shipment = pick_blocks(picks, sizes, prior_cache[0], fresh_rows, block_rows)
    decode_kv = lax.all_to_all(shipment, "req", split_axis=0, concat_axis=0, tiled=True)[None]

    attended = attention(sizes, queries, prior_cache[0], fresh_rows)
    attended, decode_kv = after(attended, decode_kv)
    gathered = lax.all_to_all(attended, "tp", split_axis=0, concat_axis=0, tiled=True)
    mixed = lax.dot_general(
        gathered.reshape(QUERY_HEAD_COUNT * HEAD_SIZE, span),
        w_out,
        (((0,), (0,)), ((), ())),
        preferred_element_type=jnp.float32,
    )
    live = rank * span + jnp.arange(span, dtype=jnp.int32) < fresh
    own = lax.dynamic_slice_in_dim(hidden_in, rank * span, span, 0).astype(jnp.float32)
    hidden_out = jnp.where(live[:, None], own + mixed, 0.0).astype(jnp.bfloat16)
    return (hidden_out, decode_kv)


def solution(mesh):
    placed = (
        P("req", None),
        P(),
        P(None, "tp"),
        P(),
        P(),
        P("req", None, None),
        P("req"),
        P("req"),
        P("req", None),
    )
    return jax.shard_map(
        shards,
        mesh=mesh,
        in_specs=placed,
        out_specs=(P(("req", "tp"), None), P(("req", "tp"), None, None, None)),
        check_vma=False,
    )
```
